128 devices in a mesh: blk: 32 (over x, z, core), mem: 4 (over y).
Axes of the slice: x: 4, y: 4, z: 4, core: 2. Of those that a mesh axis runs over, the one named last changes fastest.
Arguments:
- anomalies: bfloat16 [128, 524288], P('mem', 'blk'), may hold values from -6 to 6
- increments: bfloat16 [8, 524288], P(None, ('blk', 'mem')), may hold values from -6 to 6
- taper_table: float32 [8], replicated, may hold values from 0.2 to 1
- taper_modes: float32 [8], replicated, may hold values from 0.05 to 0.5
- pair_code: int32 [512], P(('blk', 'mem')), may hold values from 0 to 3, as said below
- pair_class: int32 [512], P(('blk', 'mem')), may hold values from 0 to 7
- pair_count: int32 [128], P(('blk', 'mem')), may hold values from 1 to 4, as said below
Outputs:
- covariance_product: float32 [8, 524288], P(None, ('blk', 'mem'))
The draws below stay inside these ranges and needn't reach their ends.
Inputs may be any that keep to these rules, and one draw needn't show every extreme that they name: `pair_code`: within one device's 4 slots the codes are distinct; slots beyond the device's count hold codes too and are not listed. `pair_count`: some device lists all 4 slots.
All inputs are finite; a program needn't handle non-finite values.
Results may differ from the reference program's by a relative error of at most 0.0029.
Values may be sent and summed in bfloat16 or wider, within the bound.
No kernel may reach another device: no remote copies, remote signals or barrier semaphores. Data moves between devices by JAX's collectives and lax.ppermute only.
A program may use at most 128 MiB of HBM per device.

```python
import math
import jax
import jax.numpy as jnp
from jax import lax

BLK_DEV = 2
BLOCK = 2048
MEMBERS = 128
COLS = 8
CLASSES = 8
MODES = 8
PCAP = 4
PERIOD = 12288
BLOCKS = 256
NV = 524288
DEVICES = 128


def draw_pair_code(key, part):
    key = jax.random.fold_in(key, 11)
    keys = jax.random.split(key, DEVICES)
    orders = jax.vmap(lambda one: jax.random.permutation(one, BLK_DEV * BLK_DEV))(keys)
    return orders[:, :PCAP].reshape(-1).astype(jnp.int32)


def draw_pair_count(key, part):
    key = jax.random.fold_in(key, 23)
    first_key, second_key = jax.random.split(key)
    counts = jax.random.randint(first_key, (DEVICES,), 1, PCAP + 1)
    fullest = jax.random.randint(second_key, (), 0, DEVICES)
    return counts.at[fullest].set(PCAP).astype(jnp.int32)


def with_ends(values, own_key, least, top_value):
    dims = values.shape
    spot = [jax.random.randint(jax.random.fold_in(own_key, axis), (), 0, dims[axis]) for axis in range(len(dims))]
    values = values.at[tuple(spot)].set(least)
    longest = dims.index(max(dims))
    spot[longest] = (spot[longest] + 1) % dims[longest]
    return values.at[tuple(spot)].set(top_value)


def block_scale(key, dims, pieces, smallest, largest):
    level, own = 1.0, jax.random.fold_in(key, 6)
    for position, shards_of in pieces:
        steps = jnp.exp(jax.random.uniform(jax.random.fold_in(own, position), (shards_of,), jnp.float32, smallest / len(pieces), largest / len(pieces)))
        level = level * jnp.repeat(steps, dims[position] // shards_of).reshape([-1 if axis == position else 1 for axis in range(len(dims))])
    return level


def normal_values(key, dims, spread, limit, cuts=(), kind=jnp.bfloat16):
    factor_of = block_scale(key, dims, cuts, -0.22, 0.18) if cuts else 1.0
    drawn = jax.random.normal(key, dims, jnp.float32) * spread * factor_of
    return jnp.minimum(jnp.maximum(drawn, -limit), limit).astype(kind)


def setup_inputs(seed: int = 0) -> dict:
    key_list = jax.random.split(jax.random.key(seed), 8)
    return {
        "anomalies": normal_values(key_list[0], (MEMBERS, NV), 1.0, 6.0, ((0, 4), (1, 32))),
        "increments": normal_values(key_list[1], (COLS, NV), 1.0, 6.0, ((1, 128),)),
        "taper_table": jnp.clip(jnp.exp(jax.random.uniform(key_list[2], (CLASSES,), jnp.float32, math.log(0.2), math.log(1.0))), 0.2, 1.0),
        "taper_modes": jnp.clip(jnp.exp(jax.random.uniform(key_list[3], (MODES,), jnp.float32, math.log(0.05), math.log(0.5))), 0.05, 0.5),
        "pair_code": draw_pair_code(jax.random.fold_in(key_list[7], 71), 0),
        "pair_class": with_ends(jax.random.randint(key_list[5], (DEVICES * PCAP,), 0, CLASSES), jax.random.fold_in(key_list[5], 1), 0, CLASSES - 1).astype(jnp.int32),
        "pair_count": draw_pair_count(jax.random.fold_in(key_list[7], 71), 0),
    }


def phases(start):
    mode_ids = jnp.arange(MODES, dtype=jnp.int32)
    places = jnp.arange(BLOCK, dtype=jnp.int32) + start
    angle = ((mode_ids[:, None] * places[None, :]) % PERIOD).astype(jnp.float32) * jnp.float32(2.0 * math.pi / PERIOD)
    return jnp.cos(angle), jnp.sin(angle)


def taper_tile(taper_modes, offset):
    hi = lax.Precision.HIGHEST
    base_cos, base_sin = phases(jnp.int32(0))
    left_basis = jnp.concatenate([base_cos * taper_modes[:, None], base_sin * taper_modes[:, None]], 0)
    far_cos, far_sin = phases(offset * BLOCK)
    right_basis = jnp.concatenate([far_cos, far_sin], 0)
    return lax.dot_general(left_basis, right_basis, (((0,), (0,)), ((), ())), precision=hi)


def reference(anomalies, increments, taper_table, taper_modes, pair_code, pair_class, pair_count):
    contract = (((0,), (0,)), ((), ()))
    ens = anomalies.reshape(MEMBERS, BLOCKS, BLOCK).transpose(1, 0, 2)
    cols = increments.reshape(COLS, BLOCKS, BLOCK).transpose(1, 0, 2)
    diag_taper = taper_tile(taper_modes, jnp.int32(0))

    def diagonal(index):
        block_x = ens[index]
        gram = lax.dot_general(block_x, block_x, contract, preferred_element_type=jnp.float32)
        tile = (gram * diag_taper).astype(jnp.bfloat16)
        return lax.dot_general(cols[index], tile, (((1,), (1,)), ((), ())), preferred_element_type=jnp.float32)

    totals = lax.map(diagonal, jnp.arange(BLOCKS, dtype=jnp.int32))
    slot = jnp.arange(DEVICES * PCAP, dtype=jnp.int32)
    owner = slot // PCAP
    listed = (slot % PCAP) < pair_count[owner]
    offset = pair_code % BLK_DEV + 1
    first = owner * BLK_DEV + pair_code // BLK_DEV
    second = (first + offset) % BLOCKS
    rho = taper_table[pair_class]

    def add_pair(acc, item):
        use, one, two, off, weight = item

        def apply(total):
            gram = lax.dot_general(ens[one], ens[two], contract, preferred_element_type=jnp.float32)
            tile = (gram * taper_tile(taper_modes, off) * weight).astype(jnp.bfloat16)
            to_first = lax.dot_general(cols[two], tile, (((1,), (1,)), ((), ())), preferred_element_type=jnp.float32)
            to_second = jnp.dot(cols[one], tile, preferred_element_type=jnp.float32)
            total = total.at[one].add(to_first)
            return total.at[two].add(to_second)

        return lax.cond(use, apply, lambda total: total, acc), None

    totals, unused = lax.scan(add_pair, totals, (listed, first, second, offset, rho))
    result = totals * jnp.float32(1.0 / (MEMBERS - 1))
    return result.transpose(1, 0, 2).reshape(COLS, NV)
```

```python
import functools
import math

import jax
import jax.numpy as jnp
import numpy as np
from jax import lax
from jax.experimental import pallas as pl
from jax.experimental.pallas import tpu as pltpu
from jax.sharding import PartitionSpec as P

BLOCK = 2048
MODES = 8
RANK = 2 * MODES
COLS = 8
LANES = 128
PERIOD = 12288
PAIR = 2
NCODE = 4
TAIL = 256
F32 = jnp.float32
BF16 = jnp.bfloat16


def basis_table():
    turn = np.outer(np.arange(MODES), np.arange(BLOCK)) % PERIOD
    angle = turn * (2.0 * math.pi / PERIOD)
    return np.concatenate([np.cos(angle), np.sin(angle)], 0).astype(np.float32)


def turn_table():
    mode = (np.arange(LANES) // COLS) % MODES
    sign = np.where(np.arange(LANES) < LANES // 2, -1.0, 1.0)
    rows = []
    for o in (1, 2):
        angle = ((mode * o * BLOCK) % PERIOD) * (2.0 * math.pi / PERIOD)
        rows += [np.cos(angle), np.sin(angle) * sign]
    rows += [np.zeros(LANES)] * 4
    return np.stack(rows).astype(np.float32)


def split(value):
    high = value.astype(BF16)
    low = (value - high.astype(F32)).astype(BF16)
    return high, low


def turned(value, turns, o, back):
    c = turns[2 * o - 2 : 2 * o - 1, :]
    s = turns[2 * o - 1 : 2 * o, :]
    other = pltpu.roll(value, LANES // 2, 1)
    return value * c - other * s if back else value * c + other * s


def message_kernel(code, klass, count, table, v_ref, out_ref):
    n = v_ref.shape[1]
    out_ref[:, :n] = v_ref[...]
    row = lax.broadcasted_iota(jnp.int32, (8, LANES), 0)
    w = jnp.zeros((8, LANES), F32)
    for slot in range(NCODE):
        rho = jnp.where(slot < count[0], table[klass[slot]], F32(0.0))
        w = w + jnp.where(row % NCODE == code[slot], rho, F32(0.0))
    high, low = split(w)
    rest = (w - high.astype(F32) - low.astype(F32)).astype(BF16)
    first = row < NCODE
    out_ref[:, n : n + LANES] = jnp.where(first, high.astype(F32), low.astype(F32)).astype(BF16)
    out_ref[:, n + LANES :] = rest


def weights_of(msg_ref):
    n = msg_ref.shape[1] - TAIL
    both = msg_ref[:, n : n + LANES].astype(F32)
    rest = msg_ref[:, n + LANES :].astype(F32)
    return both[:NCODE] + both[NCODE:] + rest[:NCODE]


def project(x, v, basis):
    wide = (basis[:, None, :] * v[None, :, :].astype(F32)).reshape(RANK * COLS, v.shape[1])
    high, low = split(wide)
    both = jnp.concatenate([high, low], 0)
    out = lax.dot_general(x, both, (((1,), (1,)), ((), ())), preferred_element_type=F32)
    return out[:, :LANES] + out[:, LANES:]


def project_kernel(x_ref, m0, m1, m2, m3, basis_ref, turns_ref, z_ref, zp_ref, um_ref, w_ref, u_sc, w_sc):
    me = lax.axis_index("mem")
    basis = basis_ref[...]
    for d, msg in enumerate((m0, m1, m2, m3)):
        src = (me + 4 - d) & 3
        w_sc[src] = weights_of(msg)
        for j in range(PAIR):
            k = src * PAIR + j
            x = x_ref[:, pl.ds(pl.multiple_of(k * BLOCK, BLOCK), BLOCK)]
            u_sc[k] = project(x, msg[:, j * BLOCK : (j + 1) * BLOCK], basis)
    turns = turns_ref[...]
    nblk = u_sc.shape[0]

    def rho(k, o):
        c = (k % PAIR) * PAIR + o - 1
        return w_sc[k // PAIR][c : c + 1, :]

    for k in range(nblk):
        z = u_sc[k]
        for o in (1, 2):
            if k + o < nblk:
                z = z + turned(u_sc[k + o], turns, o, False) * rho(k, o)
            if k - o >= 0:
                z = z + turned(u_sc[k - o], turns, o, True) * rho(k - o, o)
        z_ref[k] = z
    last = nblk - 1
    zp_ref[0] = turned(u_sc[last - 1], turns, 2, True) * rho(last - 1, 2) + turned(
        u_sc[last], turns, 1, True
    ) * rho(last, 1)
    zp_ref[1] = turned(u_sc[last], turns, 2, True) * rho(last, 2)
    um_ref[0] = u_sc[0]
    um_ref[1] = u_sc[1]
    w_ref[...] = w_sc[nblk // PAIR - 1]


def expand_kernel(modes, x_ref, z_ref, zin_ref, uin_ref, w_ref, basis_ref, turns_ref, *rest):
    outs, (z_sc, l_sc) = rest[:-2], rest[-2:]
    me = lax.axis_index("mem")
    scale = F32(1.0 / 127.0)
    for r in range(RANK):
        l_sc[r : r + 1, :] = basis_ref[r : r + 1, :] * (modes[r % MODES] * scale)
    turns = turns_ref[...]
    nblk = z_ref.shape[0]
    z_sc[...] = z_ref[...]
    z_sc[0] = z_sc[0] + zin_ref[0]
    z_sc[1] = z_sc[1] + zin_ref[1]
    last = nblk - 1
    z_sc[last - 1] = z_sc[last - 1] + turned(uin_ref[0], turns, 2, False) * w_ref[1:2, :]
    z_sc[last] = (
        z_sc[last]
        + turned(uin_ref[0], turns, 1, False) * w_ref[2:3, :]
        + turned(uin_ref[1], turns, 2, False) * w_ref[3:4, :]
    )
    left = l_sc[...]
    for d, out in enumerate(outs):
        tgt = (me + d) & 3
        for j in range(PAIR):
            k = tgt * PAIR + j
            x = x_ref[:, pl.ds(pl.multiple_of(k * BLOCK, BLOCK), BLOCK)]
            high, low = split(z_sc[k])
            t = lax.dot_general(
                jnp.concatenate([high, low], 0),
                jnp.concatenate([x, x], 0),
                (((0,), (0,)), ((), ())),
                preferred_element_type=F32,
            )
            out[:, j * BLOCK : (j + 1) * BLOCK] = jnp.sum(
                t.reshape(RANK, COLS, BLOCK) * left[:, None, :], axis=0
            )


def route(n, distance):
    return [((i - distance) % n, i) for i in range(n)]


VM = pl.BlockSpec(memory_space=pltpu.VMEM)
SM = pl.BlockSpec(memory_space=pltpu.SMEM)
LIMIT = pltpu.CompilerParams(vmem_limit_bytes=40 * 1024 * 1024)


def body(anomalies, increments, taper_table, taper_modes, pair_code, pair_class, pair_count):
    members, wide = anomalies.shape
    cols, width = increments.shape
    nmem = lax.axis_size("mem")
    nblk = wide // BLOCK
    basis = jnp.asarray(basis_table())
    turns = jnp.asarray(turn_table())
    msg = pl.pallas_call(
        message_kernel,
        out_shape=jax.ShapeDtypeStruct((cols, width + TAIL), BF16),
        in_specs=[SM, SM, SM, SM, VM],
        out_specs=VM,
        name="message",
    )(pair_code, pair_class, pair_count, taper_table, increments)
    msgs = [msg] + [lax.ppermute(msg, "mem", route(nmem, d)) for d in range(1, nmem)]
    shape = jax.ShapeDtypeStruct
    z, zp, um, w = pl.pallas_call(
        project_kernel,
        out_shape=[
            shape((nblk, members, LANES), F32),
            shape((PAIR, members, LANES), F32),
            shape((PAIR, members, LANES), F32),
            shape((NCODE, LANES), F32),
        ],
        in_specs=[VM] * 7,
        out_specs=[VM] * 4,
        scratch_shapes=[
            pltpu.VMEM((nblk, members, LANES), F32),
            pltpu.VMEM((nmem, NCODE, LANES), F32),
        ],
        compiler_params=LIMIT,
        name="project",
    )(anomalies, *msgs, basis, turns)
    nb = lax.axis_size("blk")
    zin = lax.ppermute(zp, "blk", route(nb, 1))
    uin = lax.ppermute(um, "blk", route(nb, -1))
    outs = pl.pallas_call(
        expand_kernel,
        out_shape=[shape((cols, width), F32)] * nmem,
        in_specs=[SM] + [VM] * 7,
        out_specs=[VM] * nmem,
        scratch_shapes=[
            pltpu.VMEM((nblk, members, LANES), F32),
            pltpu.VMEM((RANK, BLOCK), F32),
        ],
        compiler_params=LIMIT,
        name="expand",
    )(taper_modes, anomalies, z, zin, uin, w, basis, turns)
    total = outs[0]
    for d in range(1, nmem):
        total = total + lax.ppermute(outs[d], "mem", route(nmem, d))
    return total


def solution(mesh):
    in_specs = (
        P("mem", "blk"),
        P(None, ("blk", "mem")),
        P(),
        P(),
        P(("blk", "mem")),
        P(("blk", "mem")),
        P(("blk", "mem")),
    )
    out_specs = P(None, ("blk", "mem"))
    return jax.shard_map(body, mesh=mesh, in_specs=in_specs, out_specs=out_specs, check_vma=False)
```

```python
import functools
import math

import jax
import jax.numpy as jnp
import numpy as np
from jax import lax
from jax.experimental import pallas as pl
from jax.experimental.pallas import tpu as pltpu
from jax.sharding import PartitionSpec as P

BLOCK = 2048
MODES = 8
RANK = 2 * MODES
COLS = 8
LANES = 128
PERIOD = 12288
PAIR = 2
NCODE = 4
TAIL = 256
F32 = jnp.float32
BF16 = jnp.bfloat16


def basis_table():
    turn = np.outer(np.arange(MODES), np.arange(BLOCK)) % PERIOD
    angle = turn * (2.0 * math.pi / PERIOD)
    return np.concatenate([np.cos(angle), np.sin(angle)], 0).astype(np.float32)


def turn_table():
    mode = (np.arange(LANES) // COLS) % MODES
    sign = np.where(np.arange(LANES) < LANES // 2, -1.0, 1.0)
    rows = []
    for o in (1, 2):
        angle = ((mode * o * BLOCK) % PERIOD) * (2.0 * math.pi / PERIOD)
        rows += [np.cos(angle), np.sin(angle) * sign]
    rows += [np.zeros(LANES)] * 4
    return np.stack(rows).astype(np.float32)


def split(value):
    high = value.astype(BF16)
    low = (value - high.astype(F32)).astype(BF16)
    return high, low


def turned(value, turns, o, back):
    c = turns[2 * o - 2 : 2 * o - 1, :]
    s = turns[2 * o - 1 : 2 * o, :]
    other = pltpu.roll(value, LANES // 2, 1)
    return value * c - other * s if back else value * c + other * s


def message_kernel(code_ref, klass_ref, table_ref, v_ref, count_ref, out_ref, code, klass, table, tail, sems):
    n = v_ref.shape[1]
    body = pltpu.make_async_copy(v_ref, out_ref.at[:, :n], sems.at[0])
    body.start()
    pairs = ((code_ref, code), (klass_ref, klass), (table_ref, table))
    copies = [pltpu.make_async_copy(a, b, sems.at[i + 1]) for i, (a, b) in enumerate(pairs)]
    for c in copies:
        c.start()
    for c in copies:
        c.wait()
    row = lax.broadcasted_iota(jnp.int32, (8, LANES), 0)
    listed = jnp.broadcast_to(count_ref[...].reshape(1, 1), (8, LANES))
    w = jnp.zeros((8, LANES), F32)
    for slot in range(NCODE):
        hit = (row % NCODE == code[slot]) & (slot < listed)
        w = w + jnp.where(hit, table[klass[slot]], F32(0.0))
    high, low = split(w)
    rest = (w - high.astype(F32) - low.astype(F32)).astype(BF16)
    first = row < NCODE
    tail[:, :LANES] = jnp.where(first, high.astype(F32), low.astype(F32)).astype(BF16)
    tail[:, LANES:] = rest
    end = pltpu.make_async_copy(tail, out_ref.at[:, n:], sems.at[4])
    end.start()
    end.wait()
    body.wait()


def weights_of(msg_ref):
    n = msg_ref.shape[1] - TAIL
    both = msg_ref[:, n : n + LANES].astype(F32)
    rest = msg_ref[:, n + LANES :].astype(F32)
    return both[:NCODE] + both[NCODE:] + rest[:NCODE]


def project(x, v, basis):
    wide = (basis[:, None, :] * v[None, :, :].astype(F32)).reshape(RANK * COLS, v.shape[1])
    high, low = split(wide)
    both = jnp.concatenate([high, low], 0)
    out = lax.dot_general(x, both, (((1,), (1,)), ((), ())), preferred_element_type=F32)
    return out[:, :LANES] + out[:, LANES:]


def project_chunk(x_ref, v_ref, basis_ref, member, u_ref):
    for j in range(PAIR):
        k = member * PAIR + j
        x = x_ref[:, pl.ds(pl.multiple_of(k * BLOCK, BLOCK), BLOCK)]
        u_ref[j] = project(x, v_ref[:, j * BLOCK : (j + 1) * BLOCK], basis_ref[...])


def stage_kernel(modes, x_hbm, msg_ref, basis_ref, x_ref, l_ref, u_ref, w_ref, sem):
    copy = pltpu.make_async_copy(x_hbm, x_ref, sem)
    copy.start()
    w_ref[...] = weights_of(msg_ref)
    scale = F32(1.0 / 127.0)
    for r in range(RANK):
        l_ref[r : r + 1, :] = basis_ref[r : r + 1, :] * (modes[r % MODES] * scale)
    copy.wait()
    project_chunk(x_ref, msg_ref, basis_ref, lax.axis_index("mem"), u_ref)


def project_kernel(distance, x_ref, msg_ref, basis_ref, u_ref, w_ref):
    w_ref[...] = weights_of(msg_ref)
    project_chunk(x_ref, msg_ref, basis_ref, lax.axis_index("mem") ^ distance, u_ref)


def combine_kernel(x_ref, msg_ref, u0, u1, u2, w0, w1, w2, basis_ref, turns_ref, z_ref, e_ref, o_ref, w_ref, u_sc, w_sc):
    me = lax.axis_index("mem")
    nblk = z_ref.shape[0]
    for d, (u, w) in enumerate(((u0, w0), (u1, w1), (u2, w2))):
        for j in range(PAIR):
            u_sc[(me ^ d) * PAIR + j] = u[j]
        w_sc[me ^ d] = w[...]
    w_sc[me ^ 3] = weights_of(msg_ref)
    project_chunk(x_ref, msg_ref, basis_ref, me ^ 3, u_sc.at[pl.ds((me ^ 3) * PAIR, PAIR)])
    turns = turns_ref[...]

    def rho(k, o):
        c = (k % PAIR) * PAIR + o - 1
        return w_sc[k // PAIR][c : c + 1, :]

    last = nblk - 1
    even = lax.axis_index("blk") % 2 == 0
    ahead = (
        turned(u_sc[last - 1], turns, 2, True) * rho(last - 1, 2) + turned(u_sc[last], turns, 1, True) * rho(last, 1),
        turned(u_sc[last], turns, 2, True) * rho(last, 2),
    )
    for j in range(PAIR):
        e_ref[j] = jnp.where(even, ahead[j], u_sc[j])
        o_ref[j] = jnp.where(even, u_sc[j], ahead[j])
    for k in range(nblk):
        z = u_sc[k]
        for o in (1, 2):
            if k + o < nblk:
                z = z + turned(u_sc[k + o], turns, o, False) * rho(k, o)
            if k - o >= 0:
                z = z + turned(u_sc[k - o], turns, o, True) * rho(k - o, o)
        z_ref[k] = z
    w_ref[...] = w_sc[nblk // PAIR - 1]


def expand_kernel(x_ref, z_ref, ein_ref, oin_ref, w_ref, l_ref, turns_ref, *rest):
    outs, z_sc = rest[:-1], rest[-1]
    me = lax.axis_index("mem")
    turns = turns_ref[...]
    nblk = z_ref.shape[0]
    even = lax.axis_index("blk") % 2 == 0
    zin = [jnp.where(even, oin_ref[j], ein_ref[j]) for j in range(PAIR)]
    uin = [jnp.where(even, ein_ref[j], oin_ref[j]) for j in range(PAIR)]
    z_sc[...] = z_ref[...]
    z_sc[0] = z_sc[0] + zin[0]
    z_sc[1] = z_sc[1] + zin[1]
    last = nblk - 1
    z_sc[last - 1] = z_sc[last - 1] + turned(uin[0], turns, 2, False) * w_ref[1:2, :]
    z_sc[last] = (
        z_sc[last]
        + turned(uin[0], turns, 1, False) * w_ref[2:3, :]
        + turned(uin[1], turns, 2, False) * w_ref[3:4, :]
    )
    left = l_ref[...]
    for d, out in enumerate(outs):
        for j in range(PAIR):
            k = (me ^ d) * PAIR + j
            x = x_ref[:, pl.ds(pl.multiple_of(k * BLOCK, BLOCK), BLOCK)]
            high, low = split(z_sc[k])
            t = lax.dot_general(
                jnp.concatenate([high, low], 0),
                jnp.concatenate([x, x], 0),
                (((0,), (0,)), ((), ())),
                preferred_element_type=F32,
            )
            total = jnp.sum(t.reshape(RANK, COLS, BLOCK) * left[:, None, :], axis=0)
            out[:, j * BLOCK : (j + 1) * BLOCK] = total.astype(out.dtype)


def crossed(n, distance):
    return [(i ^ distance, i) for i in range(n)]


def partner(n, odd):
    pairs = [((2 * i + odd) % n, (2 * i + 1 + odd) % n) for i in range(n // 2)]
    return pairs + [(b, a) for a, b in pairs]


VM = pl.BlockSpec(memory_space=pltpu.VMEM)
SM = pl.BlockSpec(memory_space=pltpu.SMEM)
ANY = pl.BlockSpec(memory_space=pl.ANY)
LIMIT = pltpu.CompilerParams(vmem_limit_bytes=40 * 1024 * 1024)


def body(anomalies, increments, taper_table, taper_modes, pair_code, pair_class, pair_count):
    members, wide = anomalies.shape
    cols, width = increments.shape
    nmem = lax.axis_size("mem")
    nblk = wide // BLOCK
    basis = jnp.asarray(basis_table())
    turns = jnp.asarray(turn_table())
    shape = jax.ShapeDtypeStruct
    scalars = (pair_code, pair_class, taper_table)
    msg = pl.pallas_call(
        message_kernel,
        out_shape=shape((cols, width + TAIL), BF16),
        in_specs=[ANY] * 4 + [VM],
        out_specs=ANY,
        scratch_shapes=[pltpu.SMEM(a.shape, a.dtype) for a in scalars]
        + [pltpu.VMEM((cols, TAIL), BF16), pltpu.SemaphoreType.DMA((5,))],
        compiler_params=pltpu.CompilerParams(vmem_limit_bytes=62 * 1024 * 1024),
        name="message",
    )(*scalars, increments, pair_count)
    msgs = {d: lax.ppermute(msg, "mem", crossed(nmem, d)) for d in (3, 2, 1)}
    chunk = shape((PAIR, members, LANES), F32)
    weights = shape((NCODE, LANES), F32)
    x, left, u0, w0 = pl.pallas_call(
        stage_kernel,
        out_shape=[shape(anomalies.shape, BF16), shape(basis.shape, F32), chunk, weights],
        in_specs=[SM, ANY, VM, VM],
        out_specs=[VM] * 4,
        scratch_shapes=[pltpu.SemaphoreType.DMA],
        compiler_params=LIMIT,
        name="stage",
    )(taper_modes, anomalies, msg, basis)
    u, w = {}, {}
    for d in (1, 2):
        u[d], w[d] = pl.pallas_call(
            functools.partial(project_kernel, d),
            out_shape=[chunk, weights],
            in_specs=[VM] * 3,
            out_specs=[VM] * 2,
            compiler_params=LIMIT,
            name=f"project_{d}",
        )(x, msgs[d], basis)
    z, e, o, w3 = pl.pallas_call(
        combine_kernel,
        out_shape=[shape((nblk, members, LANES), F32), chunk, chunk, weights],
        in_specs=[VM] * 10,
        out_specs=[VM] * 4,
        scratch_shapes=[pltpu.VMEM((nblk, members, LANES), F32), pltpu.VMEM((nmem, NCODE, LANES), F32)],
        compiler_params=LIMIT,
        name="combine",
    )(x, msgs[3], u0, u[1], u[2], w0, w[1], w[2], basis, turns)
    nb = lax.axis_size("blk")
    oin = lax.ppermute(o, "blk", partner(nb, 1))
    ein = lax.ppermute(e, "blk", partner(nb, 0))
    outs = pl.pallas_call(
        expand_kernel,
        out_shape=[shape((cols, width), F32)] + [shape((cols, width), BF16)] * (nmem - 1),
        in_specs=[VM] * 7,
        out_specs=[VM] * nmem,
        scratch_shapes=[pltpu.VMEM((nblk, members, LANES), F32)],
        compiler_params=LIMIT,
        name="expand",
    )(x, z, ein, oin, w3, left, turns)
    total = outs[0]
    for d in (3, 2, 1):
        total = total + lax.ppermute(outs[d], "mem", crossed(nmem, d)).astype(F32)
    return total


def solution(mesh):
    in_specs = (
        P("mem", "blk"),
        P(None, ("blk", "mem")),
        P(),
        P(),
        P(("blk", "mem")),
        P(("blk", "mem")),
        P(("blk", "mem")),
    )
    out_specs = P(None, ("blk", "mem"))
    return jax.shard_map(body, mesh=mesh, in_specs=in_specs, out_specs=out_specs, check_vma=False)
```

```python
import functools
import math

import jax
import jax.numpy as jnp
from jax import lax
from jax.experimental import pallas as pl
from jax.experimental.pallas import tpu as pltpu
from jax.sharding import PartitionSpec as P

BLOCK = 2048
MODES = 8
RANK = 2 * MODES
COLS = 8
LANES = 128
PERIOD = 12288
PAIR = 2
NCODE = 4
TAIL = 256
F32 = jnp.float32
BF16 = jnp.bfloat16


def cosine(turn):
    turn = lax.rem(turn, jnp.int32(PERIOD))
    fold = jnp.abs(turn - PERIOD // 2) - PERIOD // 4
    x = fold.astype(F32) * F32(2.0 * math.pi / PERIOD)
    y = x * x
    total = F32(1.0 / 6227020800.0)
    for c in (-1.0 / 39916800.0, 1.0 / 362880.0, -1.0 / 5040.0, 1.0 / 120.0, -1.0 / 6.0, 1.0):
        total = total * y + F32(c)
    return x * total


def write_basis(ref):
    row = lax.broadcasted_iota(jnp.int32, (RANK, LANES), 0)
    lane = lax.broadcasted_iota(jnp.int32, (RANK, LANES), 1)
    shift = jnp.where(row < MODES, 0, PERIOD - PERIOD // 4)
    for c in range(0, BLOCK, LANES):
        ref[:, c : c + LANES] = cosine((row % MODES) * (lane + c) + shift)


def write_turns(ref):
    row = lax.broadcasted_iota(jnp.int32, (8, LANES), 0)
    lane = lax.broadcasted_iota(jnp.int32, (8, LANES), 1)
    shift = jnp.where(row % 2 == 0, 0, PERIOD - PERIOD // 4)
    value = cosine(((lane // COLS) % MODES) * ((row // 2 + 1) * BLOCK) + shift)
    ref[...] = jnp.where((row % 2 == 1) & (lane < LANES // 2), -value, value)


def split(value):
    high = value.astype(BF16)
    low = (value - high.astype(F32)).astype(BF16)
    return high, low


def turned(value, turns, o, back):
    c = turns[2 * o - 2 : 2 * o - 1, :]
    s = turns[2 * o - 1 : 2 * o, :]
    other = pltpu.roll(value, LANES // 2, 1)
    return value * c - other * s if back else value * c + other * s


def message_kernel(code, klass, count, table, modes, v_ref, out_ref, aux_ref):
    n = v_ref.shape[1]
    out_ref[:, :n] = v_ref[...]
    row = lax.broadcasted_iota(jnp.int32, (8, LANES), 0)
    w = jnp.zeros((8, LANES), F32)
    for slot in range(NCODE):
        rho = jnp.where(slot < count[0], table[klass[slot]], F32(0.0))
        w = w + jnp.where(row % NCODE == code[slot], rho, F32(0.0))
    high, low = split(w)
    rest = (w - high.astype(F32) - low.astype(F32)).astype(BF16)
    first = row < NCODE
    out_ref[:, n : n + LANES] = jnp.where(first, high.astype(F32), low.astype(F32)).astype(BF16)
    out_ref[:, n + LANES :] = rest
    aux_ref[:8, :] = w
    rank = lax.broadcasted_iota(jnp.int32, (RANK, LANES), 0) % MODES
    gain = jnp.zeros((RANK, LANES), F32)
    for m in range(MODES):
        gain = jnp.where(rank == m, modes[m] * F32(1.0 / 127.0), gain)
    aux_ref[8:, :] = gain


def weights_of(msg_ref):
    n = msg_ref.shape[1] - TAIL
    both = msg_ref[:, n : n + LANES].astype(F32)
    rest = msg_ref[:, n + LANES :].astype(F32)
    return both[:NCODE] + both[NCODE:] + rest[:NCODE]


def project(x, v, basis):
    wide = (basis[:, None, :] * v[None, :, :].astype(F32)).reshape(RANK * COLS, v.shape[1])
    high, low = split(wide)
    both = jnp.concatenate([high, low], 0)
    out = lax.dot_general(x, both, (((1,), (1,)), ((), ())), preferred_element_type=F32)
    return out[:, :LANES] + out[:, LANES:]


def project_chunk(x_ref, v_ref, basis_ref, member, u_ref):
    for j in range(PAIR):
        k = member * PAIR + j
        x = x_ref[:, pl.ds(pl.multiple_of(k * BLOCK, BLOCK), BLOCK)]
        u_ref[j] = project(x, v_ref[:, j * BLOCK : (j + 1) * BLOCK], basis_ref[...])


def own_kernel(x_ref, v_ref, u_ref, basis_ref, turns_ref):
    write_basis(basis_ref)
    write_turns(turns_ref)
    project_chunk(x_ref, v_ref, basis_ref, lax.axis_index("mem"), u_ref)


def project_kernel(distance, x_ref, msg_ref, basis_ref, u_ref):
    project_chunk(x_ref, msg_ref, basis_ref, lax.axis_index("mem") ^ distance, u_ref)


def combine_kernel(x_ref, u0, u2, u3, aux_ref, m1, m2, m3, basis_ref, turns_ref, u_ref, w_ref, e_ref, o_ref):
    me = lax.axis_index("mem")
    nblk = u_ref.shape[0]
    project_chunk(x_ref, m1, basis_ref, me ^ 1, u_ref.at[pl.ds((me ^ 1) * PAIR, PAIR)])
    for d, u in ((0, u0), (2, u2), (3, u3)):
        for j in range(PAIR):
            u_ref[(me ^ d) * PAIR + j] = u[j]
    w_ref[me] = aux_ref[:NCODE, :]
    for d, m in enumerate((m1, m2, m3), 1):
        w_ref[me ^ d] = weights_of(m)
    turns = turns_ref[...]
    last = nblk - 1
    w = w_ref[last // PAIR]
    even = lax.axis_index("blk") % 2 == 0
    ahead = (
        turned(u_ref[last - 1], turns, 2, True) * w[1:2] + turned(u_ref[last], turns, 1, True) * w[2:3],
        turned(u_ref[last], turns, 2, True) * w[3:4],
    )
    for j in range(PAIR):
        e_ref[j] = jnp.where(even, ahead[j], u_ref[j])
        o_ref[j] = jnp.where(even, u_ref[j], ahead[j])


def expand(x, z, l_ref):
    high, low = split(z)
    t = lax.dot_general(
        jnp.concatenate([high, low], 0),
        jnp.concatenate([x, x], 0),
        (((0,), (0,)), ((), ())),
        preferred_element_type=F32,
    )
    return jnp.sum(t.reshape(RANK, COLS, BLOCK) * l_ref[...][:, None, :], axis=0)


def inner_kernel(x_ref, u_ref, w_ref, aux_ref, basis_ref, turns_ref, z_ref, y_ref, l_ref):
    for c in range(0, BLOCK, LANES):
        l_ref[:, c : c + LANES] = basis_ref[:, c : c + LANES] * aux_ref[8:, :]
    nblk = u_ref.shape[0]
    turns = turns_ref[...]

    def rho(k, o):
        c = (k % PAIR) * PAIR + o - 1
        return w_ref[k // PAIR][c : c + 1, :]

    for k in range(nblk):
        z = u_ref[k]
        for o in (1, 2):
            if k + o < nblk:
                z = z + turned(u_ref[k + o], turns, o, False) * rho(k, o)
            if k - o >= 0:
                z = z + turned(u_ref[k - o], turns, o, True) * rho(k - o, o)
        if 2 <= k < nblk - 2:
            y_ref[k // PAIR - 1, :, (k % PAIR) * BLOCK : (k % PAIR + 1) * BLOCK] = expand(
                x_ref[:, k * BLOCK : (k + 1) * BLOCK], z, l_ref
            )
        else:
            z_ref[k % 4] = z


def close_kernel(x_ref, z_ref, zo_ref, ein_ref, oin_ref, w_ref, l_ref, turns_ref, yi_ref, *rest):
    outs, all_sc = rest[:-1], rest[-1]
    me = lax.axis_index("mem")
    turns = turns_ref[...]
    nblk = x_ref.shape[1] // BLOCK
    last = nblk - 1
    w = w_ref[last // PAIR]
    even = lax.axis_index("blk") % 2 == 0
    uin = [jnp.where(even, ein_ref[j], oin_ref[j]) for j in range(PAIR)]
    z = {j: jnp.where(even, zo_ref[j], z_ref[j] + ein_ref[j]) for j in range(PAIR)}
    z[last - 1] = z_ref[2] + turned(uin[0], turns, 2, False) * w[1:2]
    z[last] = z_ref[3] + turned(uin[0], turns, 1, False) * w[2:3] + turned(uin[1], turns, 2, False) * w[3:4]
    for k, value in z.items():
        where = slice((k % PAIR) * BLOCK, (k % PAIR + 1) * BLOCK)
        all_sc[k // PAIR, :, where] = expand(x_ref[:, k * BLOCK : (k + 1) * BLOCK], value, l_ref)
    all_sc[1] = yi_ref[0]
    all_sc[2] = yi_ref[1]
    for d, out in enumerate(outs):
        out[...] = all_sc[me ^ d].astype(out.dtype)


def crossed(n, distance):
    return [(i ^ distance, i) for i in range(n)]


def partner(n, odd):
    pairs = [((2 * i + odd) % n, (2 * i + 1 + odd) % n) for i in range(n // 2)]
    return pairs + [(b, a) for a, b in pairs]


VM = pl.BlockSpec(memory_space=pltpu.VMEM)
SM = pl.BlockSpec(memory_space=pltpu.SMEM)
LIMIT = pltpu.CompilerParams(vmem_limit_bytes=40 * 1024 * 1024)


def body(anomalies, increments, taper_table, taper_modes, pair_code, pair_class, pair_count):
    members, wide = anomalies.shape
    cols, width = increments.shape
    nmem = lax.axis_size("mem")
    nblk = wide // BLOCK
    shape = jax.ShapeDtypeStruct
    x = anomalies
    msg, aux = pl.pallas_call(
        message_kernel,
        out_shape=[shape((cols, width + TAIL), BF16), shape((8 + RANK, LANES), F32)],
        in_specs=[SM] * 5 + [VM],
        out_specs=[VM] * 2,
        name="message",
    )(pair_code, pair_class, pair_count, taper_table, taper_modes, increments)
    m1, m2, m3 = [lax.ppermute(msg, "mem", crossed(nmem, d)) for d in (1, 2, 3)]
    chunk = shape((PAIR, members, LANES), F32)
    table = shape((RANK, BLOCK), F32)
    u0, basis, turns = pl.pallas_call(
        own_kernel,
        out_shape=[chunk, table, shape((8, LANES), F32)],
        in_specs=[VM] * 2,
        out_specs=[VM] * 3,
        compiler_params=LIMIT,
        name="own",
    )(x, increments)
    u3, u2 = [
        pl.pallas_call(
            functools.partial(project_kernel, d),
            out_shape=chunk,
            in_specs=[VM] * 3,
            out_specs=VM,
            compiler_params=LIMIT,
            name=f"project_{d}",
        )(x, m, basis)
        for d, m in ((3, m3), (2, m2))
    ]
    uall, wall, e, o = pl.pallas_call(
        combine_kernel,
        out_shape=[shape((nblk, members, LANES), F32), shape((nmem, NCODE, LANES), F32), chunk, chunk],
        in_specs=[VM] * 10,
        out_specs=[VM] * 4,
        compiler_params=LIMIT,
        name="combine",
    )(x, u0, u2, u3, aux, m1, m2, m3, basis, turns)
    nb = lax.axis_size("blk")
    oin = lax.ppermute(o, "blk", partner(nb, 1))
    ein = lax.ppermute(e, "blk", partner(nb, 0))
    z, yi, left = pl.pallas_call(
        inner_kernel,
        out_shape=[shape((4, members, LANES), F32), shape((2, cols, width), F32), table],
        in_specs=[VM] * 6,
        out_specs=[VM] * 3,
        compiler_params=LIMIT,
        name="inner",
    )(x, uall, wall, aux, basis, turns)
    zo = z[:PAIR] + oin
    outs = pl.pallas_call(
        close_kernel,
        out_shape=[shape((cols, width), F32)] + [shape((cols, width), BF16)] * (nmem - 1),
        in_specs=[VM] * 9,
        out_specs=[VM] * nmem,
        scratch_shapes=[pltpu.VMEM((nmem, cols, width), F32)],
        compiler_params=LIMIT,
        name="close",
    )(x, z, zo, ein, oin, wall, left, turns, yi)
    total = outs[0]
    for d in (3, 2, 1):
        total = total + lax.ppermute(outs[d], "mem", crossed(nmem, d)).astype(F32)
    return total


def solution(mesh):
    in_specs = (
        P("mem", "blk"),
        P(None, ("blk", "mem")),
        P(),
        P(),
        P(("blk", "mem")),
        P(("blk", "mem")),
        P(("blk", "mem")),
    )
    out_specs = P(None, ("blk", "mem"))
    return jax.shard_map(body, mesh=mesh, in_specs=in_specs, out_specs=out_specs, check_vma=False)
```

```python
import functools
import math

import jax
import jax.numpy as jnp
from jax import lax
from jax.experimental import pallas as pl
from jax.experimental.pallas import tpu as pltpu
from jax.sharding import PartitionSpec as P

BLOCK = 2048
MODES = 8
RANK = 2 * MODES
COLS = 8
LANES = 128
PERIOD = 12288
PAIR = 2
NCODE = 4
TAIL = 256
F32 = jnp.float32
BF16 = jnp.bfloat16


def cosine(turn):
    turn = lax.rem(turn, jnp.int32(PERIOD))
    fold = jnp.abs(turn - PERIOD // 2) - PERIOD // 4
    x = fold.astype(F32) * F32(2.0 * math.pi / PERIOD)
    y = x * x
    total = F32(1.0 / 6227020800.0)
    for c in (-1.0 / 39916800.0, 1.0 / 362880.0, -1.0 / 5040.0, 1.0 / 120.0, -1.0 / 6.0, 1.0):
        total = total * y + F32(c)
    return x * total


def write_basis(ref):
    row = lax.broadcasted_iota(jnp.int32, (RANK, LANES), 0)
    lane = lax.broadcasted_iota(jnp.int32, (RANK, LANES), 1)
    shift = jnp.where(row < MODES, 0, PERIOD - PERIOD // 4)
    for c in range(0, BLOCK, LANES):
        ref[:, c : c + LANES] = cosine((row % MODES) * (lane + c) + shift)


def write_turns(ref):
    row = lax.broadcasted_iota(jnp.int32, (8, LANES), 0)
    lane = lax.broadcasted_iota(jnp.int32, (8, LANES), 1)
    shift = jnp.where(row % 2 == 0, 0, PERIOD - PERIOD // 4)
    value = cosine(((lane // COLS) % MODES) * ((row // 2 + 1) * BLOCK) + shift)
    ref[...] = jnp.where((row % 2 == 1) & (lane < LANES // 2), -value, value)


def split(value):
    high = value.astype(BF16)
    low = (value - high.astype(F32)).astype(BF16)
    return high, low


def turned(value, turns, o, back):
    c = turns[2 * o - 2 : 2 * o - 1, :]
    s = turns[2 * o - 1 : 2 * o, :]
    other = pltpu.roll(value, LANES // 2, 1)
    return value * c - other * s if back else value * c + other * s


def message_kernel(code, klass, count, table, v_ref, out_ref, w_ref):
    n = v_ref.shape[1]
    out_ref[:, :n] = v_ref[...]
    row = lax.broadcasted_iota(jnp.int32, (8, LANES), 0)
    w = jnp.zeros((8, LANES), F32)
    for slot in range(NCODE):
        rho = jnp.where(slot < count[0], table[klass[slot]], F32(0.0))
        w = w + jnp.where(row % NCODE == code[slot], rho, F32(0.0))
    high, low = split(w)
    rest = (w - high.astype(F32) - low.astype(F32)).astype(BF16)
    first = row < NCODE
    out_ref[:, n : n + LANES] = jnp.where(first, high.astype(F32), low.astype(F32)).astype(BF16)
    out_ref[:, n + LANES :] = rest
    w_ref[...] = w


def weights_of(msg_ref):
    n = msg_ref.shape[1] - TAIL
    both = msg_ref[:, n : n + LANES].astype(F32)
    rest = msg_ref[:, n + LANES :].astype(F32)
    return both[:NCODE] + both[NCODE:] + rest[:NCODE]


def project(x, v, basis):
    wide = (basis[:, None, :] * v[None, :, :].astype(F32)).reshape(RANK * COLS, v.shape[1])
    high, low = split(wide)
    both = jnp.concatenate([high, low], 0)
    out = lax.dot_general(x, both, (((1,), (1,)), ((), ())), preferred_element_type=F32)
    return out[:, :LANES] + out[:, LANES:]


def project_chunk(x_ref, v_ref, basis_ref, member, u_ref):
    for j in range(PAIR):
        k = member * PAIR + j
        x = x_ref[:, pl.ds(pl.multiple_of(k * BLOCK, BLOCK), BLOCK)]
        u_ref[j] = project(x, v_ref[:, j * BLOCK : (j + 1) * BLOCK], basis_ref[...])


def at_end():
    me = lax.axis_index("mem")
    return (me == 0) | (me == 3)


def chunk_of(u_ref, distance):
    return u_ref.at[pl.ds((lax.axis_index("mem") ^ distance) * PAIR, PAIR)]


def own_kernel(modes_ref, x_ref, v_ref, u_ref, basis_ref, turns_ref, l_ref, keep_ref, sem):
    copy = pltpu.make_async_copy(x_ref, keep_ref, sem)
    copy.start()
    write_basis(basis_ref)
    write_turns(turns_ref)
    row = lax.broadcasted_iota(jnp.int32, (RANK, MODES), 0) % MODES
    lane = lax.broadcasted_iota(jnp.int32, (RANK, MODES), 1)
    modes = modes_ref[...].reshape(1, MODES) * F32(1.0 / 127.0)
    gain = jnp.sum(jnp.where(row == lane, modes, F32(0.0)), axis=1, keepdims=True)
    l_ref[...] = basis_ref[...] * gain

    @pl.when(at_end())
    def _():
        project_chunk(x_ref, v_ref, basis_ref, lax.axis_index("mem"), u_ref)

    copy.wait()


def project_kernel(distance, ends, x_ref, msg_ref, basis_ref, u_ref):
    @pl.when(at_end() if ends else jnp.logical_not(at_end()))
    def _():
        project_chunk(x_ref, msg_ref, basis_ref, lax.axis_index("mem") ^ distance, u_ref)


def edges_kernel(x_ref, u0, u2, u3, own_ref, m1, m2, m3, basis_ref, turns_ref, u_ref, w_ref, e_ref, o_ref):
    me = lax.axis_index("mem")
    nblk = x_ref.shape[1] // BLOCK
    u_ref[...] = jnp.zeros_like(u_ref)

    def keep(d, u):
        for j in range(PAIR):
            u_ref[(me ^ d) * PAIR + j] = u[j]

    @pl.when(at_end())
    def _():
        keep(0, u0)
        keep(3, u3)

    @pl.when(jnp.logical_not(at_end()))
    def _():
        project_chunk(x_ref, m1, basis_ref, me ^ 1, chunk_of(u_ref, 1))
        keep(2, u2)

    w_ref[me] = own_ref[:NCODE, :]
    for d, m in ((1, m1), (2, m2), (3, m3)):
        w_ref[me ^ d] = weights_of(m)
    turns = turns_ref[...]
    last = nblk - 1
    w = w_ref[last // PAIR]
    even = lax.axis_index("blk") % 2 == 0
    ahead = (
        turned(u_ref[last - 1], turns, 2, True) * w[1:2] + turned(u_ref[last], turns, 1, True) * w[2:3],
        turned(u_ref[last], turns, 2, True) * w[3:4],
    )
    for j in range(PAIR):
        e_ref[j] = jnp.where(even, ahead[j], u_ref[j])
        o_ref[j] = jnp.where(even, u_ref[j], ahead[j])


def expand(x, z, l_ref):
    high, low = split(z)
    t = lax.dot_general(
        jnp.concatenate([high, low], 0),
        jnp.concatenate([x, x], 0),
        (((0,), (0,)), ((), ())),
        preferred_element_type=F32,
    )
    return jnp.sum(t.reshape(RANK, COLS, BLOCK) * l_ref[...][:, None, :], axis=0)


def inner_kernel(
    x_ref, uin_ref, v_ref, m1, m2, m3, w_ref, l_ref, basis_ref, turns_ref, z_ref, y_ref, u_ref
):
    me = lax.axis_index("mem")
    u_ref[...] = uin_ref[...]

    @pl.when(at_end())
    def _():
        for d, m in ((1, m1), (2, m2)):
            project_chunk(x_ref, m, basis_ref, me ^ d, chunk_of(u_ref, d))

    @pl.when(jnp.logical_not(at_end()))
    def _():
        for d, m in ((0, v_ref), (3, m3)):
            project_chunk(x_ref, m, basis_ref, me ^ d, chunk_of(u_ref, d))

    nblk = u_ref.shape[0]
    turns = turns_ref[...]

    def rho(k, o):
        c = (k % PAIR) * PAIR + o - 1
        return w_ref[k // PAIR][c : c + 1, :]

    for k in range(nblk):
        z = u_ref[k]
        for o in (1, 2):
            if k + o < nblk:
                z = z + turned(u_ref[k + o], turns, o, False) * rho(k, o)
            if k - o >= 0:
                z = z + turned(u_ref[k - o], turns, o, True) * rho(k - o, o)
        if 2 <= k < nblk - 2:
            y_ref[k // PAIR - 1, :, (k % PAIR) * BLOCK : (k % PAIR + 1) * BLOCK] = expand(
                x_ref[:, k * BLOCK : (k + 1) * BLOCK], z, l_ref
            )
        else:
            z_ref[k % 4] = z


def close_kernel(x_ref, z_ref, zo_ref, ein_ref, oin_ref, w_ref, l_ref, turns_ref, yi_ref, *rest):
    outs, all_sc = rest[:-1], rest[-1]
    me = lax.axis_index("mem")
    turns = turns_ref[...]
    nblk = x_ref.shape[1] // BLOCK
    last = nblk - 1
    w = w_ref[last // PAIR]
    even = lax.axis_index("blk") % 2 == 0
    uin = [jnp.where(even, ein_ref[j], oin_ref[j]) for j in range(PAIR)]
    z = {j: jnp.where(even, zo_ref[j], z_ref[j] + ein_ref[j]) for j in range(PAIR)}
    z[last - 1] = z_ref[2] + turned(uin[0], turns, 2, False) * w[1:2]
    z[last] = z_ref[3] + turned(uin[0], turns, 1, False) * w[2:3] + turned(uin[1], turns, 2, False) * w[3:4]
    for k, value in z.items():
        where = slice((k % PAIR) * BLOCK, (k % PAIR + 1) * BLOCK)
        all_sc[k // PAIR, :, where] = expand(x_ref[:, k * BLOCK : (k + 1) * BLOCK], value, l_ref)
    all_sc[1] = yi_ref[0]
    all_sc[2] = yi_ref[1]
    for d, out in enumerate(outs):
        out[...] = all_sc[me ^ d].astype(out.dtype)


def crossed(n, distance):
    return [(i ^ distance, i) for i in range(n)]


def partner(n, odd):
    pairs = [((2 * i + odd) % n, (2 * i + 1 + odd) % n) for i in range(n // 2)]
    return pairs + [(b, a) for a, b in pairs]


VM = pl.BlockSpec(memory_space=pltpu.VMEM)
SM = pl.BlockSpec(memory_space=pltpu.SMEM)
LIMIT = pltpu.CompilerParams(vmem_limit_bytes=40 * 1024 * 1024)


def body(anomalies, increments, taper_table, taper_modes, pair_code, pair_class, pair_count):
    members, wide = anomalies.shape
    cols, width = increments.shape
    nmem = lax.axis_size("mem")
    nblk = wide // BLOCK
    shape = jax.ShapeDtypeStruct
    x = anomalies
    msg, wown = pl.pallas_call(
        message_kernel,
        out_shape=[shape((cols, width + TAIL), BF16), shape((8, LANES), F32)],
        in_specs=[SM] * 4 + [VM],
        out_specs=[VM] * 2,
        compiler_params=LIMIT,
        name="message",
    )(pair_code, pair_class, pair_count, taper_table, increments)
    m2, m3, m1 = [lax.ppermute(msg, "mem", crossed(nmem, d)) for d in (2, 3, 1)]
    chunk = shape((PAIR, members, LANES), F32)
    table = shape((RANK, BLOCK), F32)
    u0, basis, turns, left, x = pl.pallas_call(
        own_kernel,
        out_shape=[chunk, table, shape((8, LANES), F32), table, shape(x.shape, x.dtype)],
        in_specs=[VM] * 3,
        out_specs=[VM] * 5,
        scratch_shapes=[pltpu.SemaphoreType.DMA],
        compiler_params=LIMIT,
        name="own",
    )(taper_modes, x, msg)
    u2, u3 = [
        pl.pallas_call(
            functools.partial(project_kernel, d, d == 3),
            out_shape=chunk,
            in_specs=[VM] * 3,
            out_specs=VM,
            compiler_params=LIMIT,
            name=f"project_{d}",
        )(x, m, basis)
        for d, m in ((2, m2), (3, m3))
    ]
    products = shape((nblk, members, LANES), F32)
    weights = shape((nmem, NCODE, LANES), F32)
    uend, wall, e, o = pl.pallas_call(
        edges_kernel,
        out_shape=[products, weights, chunk, chunk],
        in_specs=[VM] * 10,
        out_specs=[VM] * 4,
        compiler_params=LIMIT,
        name="edges",
    )(x, u0, u2, u3, wown, m1, m2, m3, basis, turns)
    nb = lax.axis_size("blk")
    oin = lax.ppermute(o, "blk", partner(nb, 1))
    ein = lax.ppermute(e, "blk", partner(nb, 0))
    z, yi = pl.pallas_call(
        inner_kernel,
        out_shape=[shape((4, members, LANES), F32), shape((2, cols, width), F32)],
        in_specs=[VM] * 10,
        out_specs=[VM] * 2,
        scratch_shapes=[pltpu.VMEM((nblk, members, LANES), F32)],
        compiler_params=LIMIT,
        name="inner",
    )(x, uend, msg, m1, m2, m3, wall, left, basis, turns)
    zo = z[:PAIR] + oin
    outs = pl.pallas_call(
        close_kernel,
        out_shape=[shape((cols, width), F32)] + [shape((cols, width), BF16)] * (nmem - 1),
        in_specs=[VM] * 9,
        out_specs=[VM] * nmem,
        scratch_shapes=[pltpu.VMEM((nmem, cols, width), F32)],
        compiler_params=LIMIT,
        name="close",
    )(x, z, zo, ein, oin, wall, left, turns, yi)
    total = outs[0]
    for d in (3, 2, 1):
        total = total + lax.ppermute(outs[d], "mem", crossed(nmem, d)).astype(F32)
    return total


def solution(mesh):
    in_specs = (
        P("mem", "blk"),
        P(None, ("blk", "mem")),
        P(),
        P(),
        P(("blk", "mem")),
        P(("blk", "mem")),
        P(("blk", "mem")),
    )
    out_specs = P(None, ("blk", "mem"))
    return jax.shard_map(body, mesh=mesh, in_specs=in_specs, out_specs=out_specs, check_vma=False)
```

```python
import functools
import math

import jax
import jax.numpy as jnp
from jax import lax
from jax.experimental import pallas as pl
from jax.experimental.pallas import tpu as pltpu
from jax.sharding import PartitionSpec as P

BLOCK = 2048
MODES = 8
RANK = 2 * MODES
COLS = 8
LANES = 128
PERIOD = 12288
PAIR = 2
NCODE = 4
TAIL = 256
F32 = jnp.float32
BF16 = jnp.bfloat16


def cosine(turn):
    turn = lax.rem(turn, jnp.int32(PERIOD))
    fold = jnp.abs(turn - PERIOD // 2) - PERIOD // 4
    x = fold.astype(F32) * F32(2.0 * math.pi / PERIOD)
    y = x * x
    total = F32(1.0 / 6227020800.0)
    for c in (-1.0 / 39916800.0, 1.0 / 362880.0, -1.0 / 5040.0, 1.0 / 120.0, -1.0 / 6.0, 1.0):
        total = total * y + F32(c)
    return x * total


def write_basis(ref):
    row = lax.broadcasted_iota(jnp.int32, (RANK, LANES), 0)
    lane = lax.broadcasted_iota(jnp.int32, (RANK, LANES), 1)
    shift = jnp.where(row < MODES, 0, PERIOD - PERIOD // 4)
    for c in range(0, BLOCK, LANES):
        ref[:, c : c + LANES] = cosine((row % MODES) * (lane + c) + shift)


def write_turns(ref):
    row = lax.broadcasted_iota(jnp.int32, (8, LANES), 0)
    lane = lax.broadcasted_iota(jnp.int32, (8, LANES), 1)
    shift = jnp.where(row % 2 == 0, 0, PERIOD - PERIOD // 4)
    value = cosine(((lane // COLS) % MODES) * ((row // 2 + 1) * BLOCK) + shift)
    ref[...] = jnp.where((row % 2 == 1) & (lane < LANES // 2), -value, value)


def split(value):
    high = value.astype(BF16)
    low = (value - high.astype(F32)).astype(BF16)
    return high, low


def turned(value, turns, o, back):
    c = turns[2 * o - 2 : 2 * o - 1, :]
    s = turns[2 * o - 1 : 2 * o, :]
    other = pltpu.roll(value, LANES // 2, 1)
    return value * c - other * s if back else value * c + other * s


def tables_kernel(code, klass, count, table, basis_ref, turns_ref, w_ref, tail_ref):
    row = lax.broadcasted_iota(jnp.int32, (8, LANES), 0)
    w = jnp.zeros((8, LANES), F32)
    for slot in range(NCODE):
        rho = jnp.where(slot < count[0], table[klass[slot]], F32(0.0))
        w = w + jnp.where(row % NCODE == code[slot], rho, F32(0.0))
    high, low = split(w)
    rest = (w - high.astype(F32) - low.astype(F32)).astype(BF16)
    tail_ref[:, :LANES] = jnp.where(row < NCODE, high.astype(F32), low.astype(F32)).astype(BF16)
    tail_ref[:, LANES:] = rest
    w_ref[...] = w
    write_basis(basis_ref)
    write_turns(turns_ref)


def message_kernel(v_ref, tail_ref, out_ref):
    n = v_ref.shape[1]
    out_ref[:, :n] = v_ref[...]
    out_ref[:, n:] = tail_ref[...]


def weights_of(msg_ref):
    n = msg_ref.shape[1] - TAIL
    both = msg_ref[:, n : n + LANES].astype(F32)
    rest = msg_ref[:, n + LANES :].astype(F32)
    return both[:NCODE] + both[NCODE:] + rest[:NCODE]


def project(x, v, basis):
    wide = (basis[:, None, :] * v[None, :, :].astype(F32)).reshape(RANK * COLS, v.shape[1])
    high, low = split(wide)
    both = jnp.concatenate([high, low], 0)
    out = lax.dot_general(x, both, (((1,), (1,)), ((), ())), preferred_element_type=F32)
    return out[:, :LANES] + out[:, LANES:]


def project_chunk(x_ref, v_ref, basis_ref, member, u_ref):
    for j in range(PAIR):
        k = member * PAIR + j
        x = x_ref[:, pl.ds(pl.multiple_of(k * BLOCK, BLOCK), BLOCK)]
        u_ref[j] = project(x, v_ref[:, j * BLOCK : (j + 1) * BLOCK], basis_ref[...])


def at_end():
    me = lax.axis_index("mem")
    return (me == 0) | (me == 3)


def chunk_of(u_ref, distance):
    return u_ref.at[pl.ds((lax.axis_index("mem") ^ distance) * PAIR, PAIR)]


def own_kernel(modes_ref, x_ref, v_ref, basis_ref, u_ref, l_ref, keep_ref, sem):
    copy = pltpu.make_async_copy(x_ref, keep_ref, sem)
    copy.start()
    row = lax.broadcasted_iota(jnp.int32, (RANK, MODES), 0) % MODES
    lane = lax.broadcasted_iota(jnp.int32, (RANK, MODES), 1)
    modes = modes_ref[...].reshape(1, MODES) * F32(1.0 / 127.0)
    gain = jnp.sum(jnp.where(row == lane, modes, F32(0.0)), axis=1, keepdims=True)
    l_ref[...] = basis_ref[...] * gain

    @pl.when(at_end())
    def _():
        project_chunk(x_ref, v_ref, basis_ref, lax.axis_index("mem"), u_ref)

    copy.wait()


def project_kernel(distance, ends, x_ref, msg_ref, basis_ref, u_ref):
    @pl.when(at_end() if ends else jnp.logical_not(at_end()))
    def _():
        project_chunk(x_ref, msg_ref, basis_ref, lax.axis_index("mem") ^ distance, u_ref)


def edges_kernel(x_ref, u0, u2, u3, own_ref, m1, m2, m3, basis_ref, turns_ref, u_ref, w_ref, e_ref, o_ref):
    me = lax.axis_index("mem")
    nblk = x_ref.shape[1] // BLOCK
    u_ref[...] = jnp.zeros_like(u_ref)

    def keep(d, u):
        for j in range(PAIR):
            u_ref[(me ^ d) * PAIR + j] = u[j]

    @pl.when(at_end())
    def _():
        keep(0, u0)
        keep(3, u3)

    @pl.when(jnp.logical_not(at_end()))
    def _():
        project_chunk(x_ref, m1, basis_ref, me ^ 1, chunk_of(u_ref, 1))
        keep(2, u2)

    w_ref[me] = own_ref[:NCODE, :]
    for d, m in ((1, m1), (2, m2), (3, m3)):
        w_ref[me ^ d] = weights_of(m)
    turns = turns_ref[...]
    last = nblk - 1
    w = w_ref[last // PAIR]
    even = lax.axis_index("blk") % 2 == 0
    ahead = (
        turned(u_ref[last - 1], turns, 2, True) * w[1:2] + turned(u_ref[last], turns, 1, True) * w[2:3],
        turned(u_ref[last], turns, 2, True) * w[3:4],
    )
    for j in range(PAIR):
        e_ref[j] = jnp.where(even, ahead[j], u_ref[j])
        o_ref[j] = jnp.where(even, u_ref[j], ahead[j])


def expand(x, z, l_ref):
    high, low = split(z)
    t = lax.dot_general(
        jnp.concatenate([high, low], 0),
        jnp.concatenate([x, x], 0),
        (((0,), (0,)), ((), ())),
        preferred_element_type=F32,
    )
    return jnp.sum(t.reshape(RANK, COLS, BLOCK) * l_ref[...][:, None, :], axis=0)


def inner_kernel(
    x_ref, uin_ref, v_ref, m1, m2, m3, w_ref, l_ref, basis_ref, turns_ref, z_ref, y_ref, u_ref
):
    me = lax.axis_index("mem")
    u_ref[...] = uin_ref[...]

    @pl.when(at_end())
    def _():
        for d, m in ((1, m1), (2, m2)):
            project_chunk(x_ref, m, basis_ref, me ^ d, chunk_of(u_ref, d))

    @pl.when(jnp.logical_not(at_end()))
    def _():
        for d, m in ((0, v_ref), (3, m3)):
            project_chunk(x_ref, m, basis_ref, me ^ d, chunk_of(u_ref, d))

    nblk = u_ref.shape[0]
    turns = turns_ref[...]

    def rho(k, o):
        c = (k % PAIR) * PAIR + o - 1
        return w_ref[k // PAIR][c : c + 1, :]

    for k in range(nblk):
        z = u_ref[k]
        for o in (1, 2):
            if k + o < nblk:
                z = z + turned(u_ref[k + o], turns, o, False) * rho(k, o)
            if k - o >= 0:
                z = z + turned(u_ref[k - o], turns, o, True) * rho(k - o, o)
        if 2 <= k < nblk - 2:
            y_ref[k // PAIR - 1, :, (k % PAIR) * BLOCK : (k % PAIR + 1) * BLOCK] = expand(
                x_ref[:, k * BLOCK : (k + 1) * BLOCK], z, l_ref
            )
        else:
            z_ref[k % 4] = z


def close_kernel(x_ref, z_ref, zo_ref, ein_ref, oin_ref, w_ref, l_ref, turns_ref, yi_ref, *rest):
    outs, all_sc = rest[:-1], rest[-1]
    me = lax.axis_index("mem")
    turns = turns_ref[...]
    nblk = x_ref.shape[1] // BLOCK
    last = nblk - 1
    w = w_ref[last // PAIR]
    even = lax.axis_index("blk") % 2 == 0
    uin = [jnp.where(even, ein_ref[j], oin_ref[j]) for j in range(PAIR)]
    z = {j: jnp.where(even, zo_ref[j], z_ref[j] + ein_ref[j]) for j in range(PAIR)}
    z[last - 1] = z_ref[2] + turned(uin[0], turns, 2, False) * w[1:2]
    z[last] = z_ref[3] + turned(uin[0], turns, 1, False) * w[2:3] + turned(uin[1], turns, 2, False) * w[3:4]
    for k, value in z.items():
        where = slice((k % PAIR) * BLOCK, (k % PAIR + 1) * BLOCK)
        all_sc[k // PAIR, :, where] = expand(x_ref[:, k * BLOCK : (k + 1) * BLOCK], value, l_ref)
    all_sc[1] = yi_ref[0]
    all_sc[2] = yi_ref[1]
    for d, out in enumerate(outs):
        out[...] = all_sc[me ^ d].astype(out.dtype)


def crossed(n, distance):
    return [(i ^ distance, i) for i in range(n)]


def partner(n, odd):
    pairs = [((2 * i + odd) % n, (2 * i + 1 + odd) % n) for i in range(n // 2)]
    return pairs + [(b, a) for a, b in pairs]


VM = pl.BlockSpec(memory_space=pltpu.VMEM)
SM = pl.BlockSpec(memory_space=pltpu.SMEM)
LIMIT = pltpu.CompilerParams(vmem_limit_bytes=40 * 1024 * 1024)


def body(anomalies, increments, taper_table, taper_modes, pair_code, pair_class, pair_count):
    members, wide = anomalies.shape
    cols, width = increments.shape
    nmem = lax.axis_size("mem")
    nblk = wide // BLOCK
    shape = jax.ShapeDtypeStruct
    x = anomalies
    table = shape((RANK, BLOCK), F32)
    basis, turns, wown, tail = pl.pallas_call(
        tables_kernel,
        out_shape=[table, shape((8, LANES), F32), shape((8, LANES), F32), shape((cols, TAIL), BF16)],
        in_specs=[SM] * 4,
        out_specs=[VM] * 4,
        compiler_params=LIMIT,
        cost_estimate=pl.CostEstimate(flops=1000000000, bytes_accessed=4000000, transcendentals=0),
        name="tables",
    )(pair_code, pair_class, pair_count, taper_table)
    msg = pl.pallas_call(
        message_kernel,
        out_shape=shape((cols, width + TAIL), BF16),
        in_specs=[VM] * 2,
        out_specs=VM,
        compiler_params=LIMIT,
        name="message",
    )(increments, tail)
    m2, m3, m1 = [lax.ppermute(msg, "mem", crossed(nmem, d)) for d in (2, 3, 1)]
    chunk = shape((PAIR, members, LANES), F32)
    u0, left, x = pl.pallas_call(
        own_kernel,
        out_shape=[chunk, table, shape(x.shape, x.dtype)],
        in_specs=[VM] * 4,
        out_specs=[VM] * 3,
        scratch_shapes=[pltpu.SemaphoreType.DMA],
        compiler_params=LIMIT,
        name="own",
    )(taper_modes, x, msg, basis)
    u2, u3 = [
        pl.pallas_call(
            functools.partial(project_kernel, d, d == 3),
            out_shape=chunk,
            in_specs=[VM] * 3,
            out_specs=VM,
            compiler_params=LIMIT,
            name=f"project_{d}",
        )(x, m, basis)
        for d, m in ((2, m2), (3, m3))
    ]
    products = shape((nblk, members, LANES), F32)
    weights = shape((nmem, NCODE, LANES), F32)
    uend, wall, e, o = pl.pallas_call(
        edges_kernel,
        out_shape=[products, weights, chunk, chunk],
        in_specs=[VM] * 10,
        out_specs=[VM] * 4,
        compiler_params=LIMIT,
        name="edges",
    )(x, u0, u2, u3, wown, m1, m2, m3, basis, turns)
    nb = lax.axis_size("blk")
    oin = lax.ppermute(o, "blk", partner(nb, 1))
    ein = lax.ppermute(e, "blk", partner(nb, 0))
    z, yi = pl.pallas_call(
        inner_kernel,
        out_shape=[shape((4, members, LANES), F32), shape((2, cols, width), F32)],
        in_specs=[VM] * 10,
        out_specs=[VM] * 2,
        scratch_shapes=[pltpu.VMEM((nblk, members, LANES), F32)],
        compiler_params=LIMIT,
        name="inner",
    )(x, uend, msg, m1, m2, m3, wall, left, basis, turns)
    zo = z[:PAIR] + oin
    outs = pl.pallas_call(
        close_kernel,
        out_shape=[shape((cols, width), F32)] + [shape((cols, width), BF16)] * (nmem - 1),
        in_specs=[VM] * 9,
        out_specs=[VM] * nmem,
        scratch_shapes=[pltpu.VMEM((nmem, cols, width), F32)],
        compiler_params=LIMIT,
        name="close",
    )(x, z, zo, ein, oin, wall, left, turns, yi)
    total = outs[0]
    for d in (3, 2, 1):
        total = total + lax.ppermute(outs[d], "mem", crossed(nmem, d)).astype(F32)
    return total


def solution(mesh):
    in_specs = (
        P("mem", "blk"),
        P(None, ("blk", "mem")),
        P(),
        P(),
        P(("blk", "mem")),
        P(("blk", "mem")),
        P(("blk", "mem")),
    )
    out_specs = P(None, ("blk", "mem"))
    return jax.shard_map(body, mesh=mesh, in_specs=in_specs, out_specs=out_specs, check_vma=False)
```

```python
import functools
import math

import jax
import jax.numpy as jnp
from jax import lax
from jax.experimental import pallas as pl
from jax.experimental.pallas import tpu as pltpu
from jax.sharding import PartitionSpec as P

BLOCK = 2048
MODES = 8
RANK = 2 * MODES
COLS = 8
LANES = 128
PERIOD = 12288
PAIR = 2
NCODE = 4
TAIL = 256
F32 = jnp.float32
BF16 = jnp.bfloat16


def cosine(turn):
    turn = lax.rem(turn, jnp.int32(PERIOD))
    fold = jnp.abs(turn - PERIOD // 2) - PERIOD // 4
    x = fold.astype(F32) * F32(2.0 * math.pi / PERIOD)
    y = x * x
    total = F32(1.0 / 6227020800.0)
    for c in (-1.0 / 39916800.0, 1.0 / 362880.0, -1.0 / 5040.0, 1.0 / 120.0, -1.0 / 6.0, 1.0):
        total = total * y + F32(c)
    return x * total


def write_basis(ref):
    row = lax.broadcasted_iota(jnp.int32, (RANK, LANES), 0)
    lane = lax.broadcasted_iota(jnp.int32, (RANK, LANES), 1)
    shift = jnp.where(row < MODES, 0, PERIOD - PERIOD // 4)
    for c in range(0, BLOCK, LANES):
        ref[:, c : c + LANES] = cosine((row % MODES) * (lane + c) + shift)


def write_turns(ref):
    row = lax.broadcasted_iota(jnp.int32, (8, LANES), 0)
    lane = lax.broadcasted_iota(jnp.int32, (8, LANES), 1)
    shift = jnp.where(row % 2 == 0, 0, PERIOD - PERIOD // 4)
    value = cosine(((lane // COLS) % MODES) * ((row // 2 + 1) * BLOCK) + shift)
    ref[...] = jnp.where((row % 2 == 1) & (lane < LANES // 2), -value, value)


def split(value):
    high = value.astype(BF16)
    low = (value - high.astype(F32)).astype(BF16)
    return high, low


def turned(value, turns, o, back):
    c = turns[2 * o - 2 : 2 * o - 1, :]
    s = turns[2 * o - 1 : 2 * o, :]
    other = pltpu.roll(value, LANES // 2, 1)
    return value * c - other * s if back else value * c + other * s


def tables_kernel(code, klass, count, table, basis_ref, turns_ref, w_ref, tail_ref):
    row = lax.broadcasted_iota(jnp.int32, (8, LANES), 0)
    w = jnp.zeros((8, LANES), F32)
    for slot in range(NCODE):
        rho = jnp.where(slot < count[0], table[klass[slot]], F32(0.0))
        w = w + jnp.where(row % NCODE == code[slot], rho, F32(0.0))
    high, low = split(w)
    rest = (w - high.astype(F32) - low.astype(F32)).astype(BF16)
    tail_ref[:, :LANES] = jnp.where(row < NCODE, high.astype(F32), low.astype(F32)).astype(BF16)
    tail_ref[:, LANES:] = rest
    w_ref[...] = w
    write_basis(basis_ref)
    write_turns(turns_ref)


def message_kernel(v_ref, tail_ref, out_ref):
    n = v_ref.shape[1]
    out_ref[:, :n] = v_ref[...]
    out_ref[:, n:] = tail_ref[...]


def weights_of(msg_ref):
    n = msg_ref.shape[1] - TAIL
    both = msg_ref[:, n : n + LANES].astype(F32)
    rest = msg_ref[:, n + LANES :].astype(F32)
    return both[:NCODE] + both[NCODE:] + rest[:NCODE]


def project(x, v, basis):
    wide = (basis[:, None, :] * v[None, :, :].astype(F32)).reshape(RANK * COLS, v.shape[1])
    high, low = split(wide)
    both = jnp.concatenate([high, low], 0)
    out = lax.dot_general(x, both, (((1,), (1,)), ((), ())), preferred_element_type=F32)
    return out[:, :LANES] + out[:, LANES:]


def project_chunk(x_ref, v_ref, basis_ref, member, u_ref):
    for j in range(PAIR):
        k = member * PAIR + j
        x = x_ref[:, pl.ds(pl.multiple_of(k * BLOCK, BLOCK), BLOCK)]
        u_ref[j] = project(x, v_ref[:, j * BLOCK : (j + 1) * BLOCK], basis_ref[...])


def at_end():
    me = lax.axis_index("mem")
    return (me == 0) | (me == 3)


def chunk_of(u_ref, distance):
    return u_ref.at[pl.ds((lax.axis_index("mem") ^ distance) * PAIR, PAIR)]


def own_kernel(modes_ref, x_ref, v_ref, basis_ref, u_ref, l_ref, keep_ref, sem):
    copy = pltpu.make_async_copy(x_ref, keep_ref, sem)
    copy.start()
    row = lax.broadcasted_iota(jnp.int32, (RANK, MODES), 0) % MODES
    lane = lax.broadcasted_iota(jnp.int32, (RANK, MODES), 1)
    modes = modes_ref[...].reshape(1, MODES) * F32(1.0 / 127.0)
    gain = jnp.sum(jnp.where(row == lane, modes, F32(0.0)), axis=1, keepdims=True)
    l_ref[...] = basis_ref[...] * gain

    project_chunk(x_ref, v_ref, basis_ref, lax.axis_index("mem"), u_ref)
    copy.wait()


def project_kernel(distance, every, x_ref, msg_ref, basis_ref, u_ref):
    @pl.when(every | jnp.logical_not(at_end()))
    def _():
        project_chunk(x_ref, msg_ref, basis_ref, lax.axis_index("mem") ^ distance, u_ref)


def one_needed():
    even = lax.axis_index("blk") % 2 == 0
    return lax.axis_index("mem") == jnp.where(even, 1, 2)


def piece(target, parts):
    d = lax.axis_index("mem") ^ target
    found = [parts[0][j] for j in range(PAIR)]
    for k in range(1, len(parts)):
        found = [jnp.where(d == k, parts[k][j], found[j]) for j in range(PAIR)]
    return found


def ahead_of(high, w, turns):
    return (
        turned(high[0], turns, 2, True) * w[1:2] + turned(high[1], turns, 1, True) * w[2:3],
        turned(high[1], turns, 2, True) * w[3:4],
    )


def outward_kernel(x_ref, u0, u2, u3, own_ref, m1, m2, m3, basis_ref, turns_ref, u1_ref, w_ref, o_ref):
    me = lax.axis_index("mem")
    u1_ref[...] = jnp.zeros_like(u1_ref)

    @pl.when(one_needed())
    def _():
        project_chunk(x_ref, m1, basis_ref, me ^ 1, u1_ref)

    w_ref[me] = own_ref[:NCODE, :]
    for d, m in ((1, m1), (2, m2), (3, m3)):
        w_ref[me ^ d] = weights_of(m)
    even = lax.axis_index("blk") % 2 == 0
    parts = (u0, u1_ref, u2, u3)
    ahead = ahead_of(piece(3, parts), w_ref[3], turns_ref[...])
    low = piece(0, parts)
    for j in range(PAIR):
        o_ref[j] = jnp.where(even, low[j], ahead[j])


def inward_kernel(x_ref, u0, u1, u2, u3, m1, w_ref, basis_ref, turns_ref, u_ref, e_ref):
    me = lax.axis_index("mem")
    for d, u in enumerate((u0, u1, u2, u3)):
        for j in range(PAIR):
            u_ref[(me ^ d) * PAIR + j] = u[j]

    @pl.when(jnp.logical_not(at_end() | one_needed()))
    def _():
        project_chunk(x_ref, m1, basis_ref, me ^ 1, chunk_of(u_ref, 1))

    even = lax.axis_index("blk") % 2 == 0
    last = u_ref.shape[0] - 1
    ahead = ahead_of((u_ref[last - 1], u_ref[last]), w_ref[3], turns_ref[...])
    for j in range(PAIR):
        e_ref[j] = jnp.where(even, ahead[j], u_ref[j])


def expand(x, z, l_ref):
    high, low = split(z)
    t = lax.dot_general(
        jnp.concatenate([high, low], 0),
        jnp.concatenate([x, x], 0),
        (((0,), (0,)), ((), ())),
        preferred_element_type=F32,
    )
    return jnp.sum(t.reshape(RANK, COLS, BLOCK) * l_ref[...][:, None, :], axis=0)


def inner_kernel(
    x_ref, uin_ref, m1, m2, w_ref, l_ref, basis_ref, turns_ref, z_ref, y_ref, u_ref
):
    me = lax.axis_index("mem")
    u_ref[...] = uin_ref[...]

    @pl.when(at_end())
    def _():
        for d, m in ((1, m1), (2, m2)):
            project_chunk(x_ref, m, basis_ref, me ^ d, chunk_of(u_ref, d))

    nblk = u_ref.shape[0]
    turns = turns_ref[...]

    def rho(k, o):
        c = (k % PAIR) * PAIR + o - 1
        return w_ref[k // PAIR][c : c + 1, :]

    for k in range(nblk):
        z = u_ref[k]
        for o in (1, 2):
            if k + o < nblk:
                z = z + turned(u_ref[k + o], turns, o, False) * rho(k, o)
            if k - o >= 0:
                z = z + turned(u_ref[k - o], turns, o, True) * rho(k - o, o)
        if 2 <= k < nblk - 2:
            y_ref[k // PAIR - 1, :, (k % PAIR) * BLOCK : (k % PAIR + 1) * BLOCK] = expand(
                x_ref[:, k * BLOCK : (k + 1) * BLOCK], z, l_ref
            )
        else:
            z_ref[k % 4] = z


def close_kernel(x_ref, z_ref, zo_ref, ein_ref, oin_ref, w_ref, l_ref, turns_ref, yi_ref, *rest):
    outs, all_sc = rest[:-1], rest[-1]
    me = lax.axis_index("mem")
    turns = turns_ref[...]
    nblk = x_ref.shape[1] // BLOCK
    last = nblk - 1
    w = w_ref[last // PAIR]
    even = lax.axis_index("blk") % 2 == 0
    uin = [jnp.where(even, ein_ref[j], oin_ref[j]) for j in range(PAIR)]
    z = {j: jnp.where(even, zo_ref[j], z_ref[j] + ein_ref[j]) for j in range(PAIR)}
    z[last - 1] = z_ref[2] + turned(uin[0], turns, 2, False) * w[1:2]
    z[last] = z_ref[3] + turned(uin[0], turns, 1, False) * w[2:3] + turned(uin[1], turns, 2, False) * w[3:4]
    for k, value in z.items():
        where = slice((k % PAIR) * BLOCK, (k % PAIR + 1) * BLOCK)
        all_sc[k // PAIR, :, where] = expand(x_ref[:, k * BLOCK : (k + 1) * BLOCK], value, l_ref)
    all_sc[1] = yi_ref[0]
    all_sc[2] = yi_ref[1]
    for d, out in enumerate(outs):
        out[...] = all_sc[me ^ d].astype(out.dtype)


def crossed(n, distance):
    return [(i ^ distance, i) for i in range(n)]


def partner(n, odd):
    pairs = [((2 * i + odd) % n, (2 * i + 1 + odd) % n) for i in range(n // 2)]
    return pairs + [(b, a) for a, b in pairs]


VM = pl.BlockSpec(memory_space=pltpu.VMEM)
SM = pl.BlockSpec(memory_space=pltpu.SMEM)
LIMIT = pltpu.CompilerParams(vmem_limit_bytes=40 * 1024 * 1024)


def body(anomalies, increments, taper_table, taper_modes, pair_code, pair_class, pair_count):
    members, wide = anomalies.shape
    cols, width = increments.shape
    nmem = lax.axis_size("mem")
    nblk = wide // BLOCK
    shape = jax.ShapeDtypeStruct
    x = anomalies
    table = shape((RANK, BLOCK), F32)
    basis, turns, wown, tail = pl.pallas_call(
        tables_kernel,
        out_shape=[table, shape((8, LANES), F32), shape((8, LANES), F32), shape((cols, TAIL), BF16)],
        in_specs=[SM] * 4,
        out_specs=[VM] * 4,
        compiler_params=LIMIT,
        cost_estimate=pl.CostEstimate(flops=1000000000, bytes_accessed=4000000, transcendentals=0),
        name="tables",
    )(pair_code, pair_class, pair_count, taper_table)
    msg = pl.pallas_call(
        message_kernel,
        out_shape=shape((cols, width + TAIL), BF16),
        in_specs=[VM] * 2,
        out_specs=VM,
        compiler_params=LIMIT,
        name="message",
    )(increments, tail)
    m2, m3, m1 = [lax.ppermute(msg, "mem", crossed(nmem, d)) for d in (2, 3, 1)]
    chunk = shape((PAIR, members, LANES), F32)
    u0, left, x = pl.pallas_call(
        own_kernel,
        out_shape=[chunk, table, shape(x.shape, x.dtype)],
        in_specs=[VM] * 4,
        out_specs=[VM] * 3,
        scratch_shapes=[pltpu.SemaphoreType.DMA],
        compiler_params=LIMIT,
        name="own",
    )(taper_modes, x, msg, basis)
    u2, u3 = [
        pl.pallas_call(
            functools.partial(project_kernel, d, d == 3),
            out_shape=chunk,
            in_specs=[VM] * 3,
            out_specs=VM,
            compiler_params=LIMIT,
            name=f"project_{d}",
        )(x, m, basis)
        for d, m in ((2, m2), (3, m3))
    ]
    products = shape((nblk, members, LANES), F32)
    weights = shape((nmem, NCODE, LANES), F32)
    u1, wall, o = pl.pallas_call(
        outward_kernel,
        out_shape=[chunk, weights, chunk],
        in_specs=[VM] * 10,
        out_specs=[VM] * 3,
        compiler_params=LIMIT,
        name="outward",
    )(x, u0, u2, u3, wown, m1, m2, m3, basis, turns)
    uend, e = pl.pallas_call(
        inward_kernel,
        out_shape=[products, chunk],
        in_specs=[VM] * 9,
        out_specs=[VM] * 2,
        compiler_params=LIMIT,
        name="inward",
    )(x, u0, u1, u2, u3, m1, wall, basis, turns)
    nb = lax.axis_size("blk")
    oin = lax.ppermute(o, "blk", partner(nb, 1))
    ein = lax.ppermute(e, "blk", partner(nb, 0))
    z, yi = pl.pallas_call(
        inner_kernel,
        out_shape=[shape((4, members, LANES), F32), shape((2, cols, width), F32)],
        in_specs=[VM] * 8,
        out_specs=[VM] * 2,
        scratch_shapes=[pltpu.VMEM((nblk, members, LANES), F32)],
        compiler_params=LIMIT,
        name="inner",
    )(x, uend, m1, m2, wall, left, basis, turns)
    zo = z[:PAIR] + oin
    outs = pl.pallas_call(
        close_kernel,
        out_shape=[shape((cols, width), F32)] + [shape((cols, width), BF16)] * (nmem - 1),
        in_specs=[VM] * 9,
        out_specs=[VM] * nmem,
        scratch_shapes=[pltpu.VMEM((nmem, cols, width), F32)],
        compiler_params=LIMIT,
        name="close",
    )(x, z, zo, ein, oin, wall, left, turns, yi)
    total = outs[0]
    for d in (3, 2, 1):
        total = total + lax.ppermute(outs[d], "mem", crossed(nmem, d)).astype(F32)
    return total


def solution(mesh):
    in_specs = (
        P("mem", "blk"),
        P(None, ("blk", "mem")),
        P(),
        P(),
        P(("blk", "mem")),
        P(("blk", "mem")),
        P(("blk", "mem")),
    )
    out_specs = P(None, ("blk", "mem"))
    return jax.shard_map(body, mesh=mesh, in_specs=in_specs, out_specs=out_specs, check_vma=False)
```

```python
import functools
import math

import jax
import jax.numpy as jnp
from jax import lax
from jax.experimental import pallas as pl
from jax.experimental.pallas import tpu as pltpu
from jax.sharding import PartitionSpec as P

BLOCK = 2048
MODES = 8
RANK = 2 * MODES
COLS = 8
LANES = 128
PERIOD = 12288
PAIR = 2
NCODE = 4
TAIL = 256
F32 = jnp.float32
BF16 = jnp.bfloat16


def cosine(turn):
    turn = lax.rem(turn, jnp.int32(PERIOD))
    fold = jnp.abs(turn - PERIOD // 2) - PERIOD // 4
    x = fold.astype(F32) * F32(2.0 * math.pi / PERIOD)
    y = x * x
    total = F32(1.0 / 6227020800.0)
    for c in (-1.0 / 39916800.0, 1.0 / 362880.0, -1.0 / 5040.0, 1.0 / 120.0, -1.0 / 6.0, 1.0):
        total = total * y + F32(c)
    return x * total


def write_basis(ref):
    row = lax.broadcasted_iota(jnp.int32, (RANK, LANES), 0)
    lane = lax.broadcasted_iota(jnp.int32, (RANK, LANES), 1)
    shift = jnp.where(row < MODES, 0, PERIOD - PERIOD // 4)
    for c in range(0, BLOCK, LANES):
        ref[:, c : c + LANES] = cosine((row % MODES) * (lane + c) + shift)


def write_turns(ref):
    row = lax.broadcasted_iota(jnp.int32, (8, LANES), 0)
    lane = lax.broadcasted_iota(jnp.int32, (8, LANES), 1)
    shift = jnp.where(row % 2 == 0, 0, PERIOD - PERIOD // 4)
    value = cosine(((lane // COLS) % MODES) * ((row // 2 + 1) * BLOCK) + shift)
    ref[...] = jnp.where((row % 2 == 1) & (lane < LANES // 2), -value, value)


def split(value):
    high = value.astype(BF16)
    low = (value - high.astype(F32)).astype(BF16)
    return high, low


def turned(value, turns, o, back):
    c = turns[2 * o - 2 : 2 * o - 1, :]
    s = turns[2 * o - 1 : 2 * o, :]
    other = pltpu.roll(value, LANES // 2, 1)
    return value * c - other * s if back else value * c + other * s


def tables_kernel(code, klass, count, table, basis_ref, turns_ref, w_ref, tail_ref):
    row = lax.broadcasted_iota(jnp.int32, (8, LANES), 0)
    w = jnp.zeros((8, LANES), F32)
    for slot in range(NCODE):
        rho = jnp.where(slot < count[0], table[klass[slot]], F32(0.0))
        w = w + jnp.where(row % NCODE == code[slot], rho, F32(0.0))
    high, low = split(w)
    rest = (w - high.astype(F32) - low.astype(F32)).astype(BF16)
    tail_ref[:, :LANES] = jnp.where(row < NCODE, high.astype(F32), low.astype(F32)).astype(BF16)
    tail_ref[:, LANES:] = rest
    w_ref[...] = w
    write_basis(basis_ref)
    write_turns(turns_ref)


def message_kernel(v_ref, tail_ref, out_ref):
    n = v_ref.shape[1]
    out_ref[:, :n] = v_ref[...]
    out_ref[:, n:] = tail_ref[...]


def weights_of(msg_ref):
    n = msg_ref.shape[1] - TAIL
    both = msg_ref[:, n : n + LANES].astype(F32)
    rest = msg_ref[:, n + LANES :].astype(F32)
    return both[:NCODE] + both[NCODE:] + rest[:NCODE]


def project(x, v, basis):
    wide = (basis[:, None, :] * v[None, :, :].astype(F32)).reshape(RANK * COLS, v.shape[1])
    high, low = split(wide)
    both = jnp.concatenate([high, low], 0)
    out = lax.dot_general(x, both, (((1,), (1,)), ((), ())), preferred_element_type=F32)
    return out[:, :LANES] + out[:, LANES:]


def project_chunk(x_ref, v_ref, basis_ref, member, u_ref):
    for j in range(PAIR):
        k = member * PAIR + j
        x = x_ref[:, pl.ds(pl.multiple_of(k * BLOCK, BLOCK), BLOCK)]
        u_ref[j] = project(x, v_ref[:, j * BLOCK : (j + 1) * BLOCK], basis_ref[...])


def at_end():
    me = lax.axis_index("mem")
    return (me == 0) | (me == 3)


def chunk_of(u_ref, distance):
    return u_ref.at[pl.ds((lax.axis_index("mem") ^ distance) * PAIR, PAIR)]


def own_kernel(modes_ref, x_ref, v_ref, basis_ref, u_ref, l_ref, keep_ref, sem):
    copy = pltpu.make_async_copy(x_ref, keep_ref, sem)
    copy.start()
    row = lax.broadcasted_iota(jnp.int32, (RANK, MODES), 0) % MODES
    lane = lax.broadcasted_iota(jnp.int32, (RANK, MODES), 1)
    modes = modes_ref[...].reshape(1, MODES) * F32(1.0 / 127.0)
    gain = jnp.sum(jnp.where(row == lane, modes, F32(0.0)), axis=1, keepdims=True)
    l_ref[...] = basis_ref[...] * gain

    project_chunk(x_ref, v_ref, basis_ref, lax.axis_index("mem"), u_ref)
    copy.wait()


def project_kernel(distance, every, x_ref, msg_ref, basis_ref, u_ref):
    @pl.when(every | jnp.logical_not(at_end()))
    def _():
        project_chunk(x_ref, msg_ref, basis_ref, lax.axis_index("mem") ^ distance, u_ref)


def edges_kernel(x_ref, u0, u2, u3, own_ref, m1, m2, m3, basis_ref, turns_ref, u_ref, w_ref, e_ref, o_ref):
    me = lax.axis_index("mem")
    nblk = x_ref.shape[1] // BLOCK
    u_ref[...] = jnp.zeros_like(u_ref)

    def keep(d, u):
        for j in range(PAIR):
            u_ref[(me ^ d) * PAIR + j] = u[j]

    keep(0, u0)
    keep(3, u3)

    @pl.when(jnp.logical_not(at_end()))
    def _():
        project_chunk(x_ref, m1, basis_ref, me ^ 1, chunk_of(u_ref, 1))
        keep(2, u2)

    w_ref[me] = own_ref[:NCODE, :]
    for d, m in ((1, m1), (2, m2), (3, m3)):
        w_ref[me ^ d] = weights_of(m)
    turns = turns_ref[...]
    last = nblk - 1
    w = w_ref[last // PAIR]
    even = lax.axis_index("blk") % 2 == 0
    ahead = (
        turned(u_ref[last - 1], turns, 2, True) * w[1:2] + turned(u_ref[last], turns, 1, True) * w[2:3],
        turned(u_ref[last], turns, 2, True) * w[3:4],
    )
    for j in range(PAIR):
        e_ref[j] = jnp.where(even, ahead[j], u_ref[j])
        o_ref[j] = jnp.where(even, u_ref[j], ahead[j])


def expand(x, z, l_ref):
    high, low = split(z)
    t = lax.dot_general(
        jnp.concatenate([high, low], 0),
        jnp.concatenate([x, x], 0),
        (((0,), (0,)), ((), ())),
        preferred_element_type=F32,
    )
    return jnp.sum(t.reshape(RANK, COLS, BLOCK) * l_ref[...][:, None, :], axis=0)


def inner_kernel(
    x_ref, uin_ref, m1, m2, w_ref, l_ref, basis_ref, turns_ref, z_ref, y_ref, u_ref
):
    me = lax.axis_index("mem")
    u_ref[...] = uin_ref[...]

    @pl.when(at_end())
    def _():
        for d, m in ((1, m1), (2, m2)):
            project_chunk(x_ref, m, basis_ref, me ^ d, chunk_of(u_ref, d))

    nblk = u_ref.shape[0]
    turns = turns_ref[...]

    def rho(k, o):
        c = (k % PAIR) * PAIR + o - 1
        return w_ref[k // PAIR][c : c + 1, :]

    for k in range(nblk):
        z = u_ref[k]
        for o in (1, 2):
            if k + o < nblk:
                z = z + turned(u_ref[k + o], turns, o, False) * rho(k, o)
            if k - o >= 0:
                z = z + turned(u_ref[k - o], turns, o, True) * rho(k - o, o)
        if 2 <= k < nblk - 2:
            y_ref[k // PAIR - 1, :, (k % PAIR) * BLOCK : (k % PAIR + 1) * BLOCK] = expand(
                x_ref[:, k * BLOCK : (k + 1) * BLOCK], z, l_ref
            )
        else:
            z_ref[k % 4] = z


def close_kernel(x_ref, z_ref, zo_ref, ein_ref, oin_ref, w_ref, l_ref, turns_ref, yi_ref, *rest):
    outs, all_sc = rest[:-1], rest[-1]
    me = lax.axis_index("mem")
    turns = turns_ref[...]
    nblk = x_ref.shape[1] // BLOCK
    last = nblk - 1
    w = w_ref[last // PAIR]
    even = lax.axis_index("blk") % 2 == 0
    uin = [jnp.where(even, ein_ref[j], oin_ref[j]) for j in range(PAIR)]
    z = {j: jnp.where(even, zo_ref[j], z_ref[j] + ein_ref[j]) for j in range(PAIR)}
    z[last - 1] = z_ref[2] + turned(uin[0], turns, 2, False) * w[1:2]
    z[last] = z_ref[3] + turned(uin[0], turns, 1, False) * w[2:3] + turned(uin[1], turns, 2, False) * w[3:4]
    for k, value in z.items():
        where = slice((k % PAIR) * BLOCK, (k % PAIR + 1) * BLOCK)
        all_sc[k // PAIR, :, where] = expand(x_ref[:, k * BLOCK : (k + 1) * BLOCK], value, l_ref)
    all_sc[1] = yi_ref[0]
    all_sc[2] = yi_ref[1]
    for d, out in enumerate(outs):
        out[...] = all_sc[me ^ d].astype(out.dtype)


def crossed(n, distance):
    return [(i ^ distance, i) for i in range(n)]


def partner(n, odd):
    pairs = [((2 * i + odd) % n, (2 * i + 1 + odd) % n) for i in range(n // 2)]
    return pairs + [(b, a) for a, b in pairs]


VM = pl.BlockSpec(memory_space=pltpu.VMEM)
SM = pl.BlockSpec(memory_space=pltpu.SMEM)
LIMIT = pltpu.CompilerParams(vmem_limit_bytes=40 * 1024 * 1024)


def body(anomalies, increments, taper_table, taper_modes, pair_code, pair_class, pair_count):
    members, wide = anomalies.shape
    cols, width = increments.shape
    nmem = lax.axis_size("mem")
    nblk = wide // BLOCK
    shape = jax.ShapeDtypeStruct
    x = anomalies
    table = shape((RANK, BLOCK), F32)
    basis, turns, wown, tail = pl.pallas_call(
        tables_kernel,
        out_shape=[table, shape((8, LANES), F32), shape((8, LANES), F32), shape((cols, TAIL), BF16)],
        in_specs=[SM] * 4,
        out_specs=[VM] * 4,
        compiler_params=LIMIT,
        cost_estimate=pl.CostEstimate(flops=1000000000, bytes_accessed=4000000, transcendentals=0),
        name="tables",
    )(pair_code, pair_class, pair_count, taper_table)
    msg = pl.pallas_call(
        message_kernel,
        out_shape=shape((cols, width + TAIL), BF16),
        in_specs=[VM] * 2,
        out_specs=VM,
        compiler_params=LIMIT,
        name="message",
    )(increments, tail)
    m2, m3, m1 = [lax.ppermute(msg, "mem", crossed(nmem, d)) for d in (2, 3, 1)]
    chunk = shape((PAIR, members, LANES), F32)
    u0, left, x = pl.pallas_call(
        own_kernel,
        out_shape=[chunk, table, shape(x.shape, x.dtype)],
        in_specs=[VM] * 4,
        out_specs=[VM] * 3,
        scratch_shapes=[pltpu.SemaphoreType.DMA],
        compiler_params=LIMIT,
        name="own",
    )(taper_modes, x, msg, basis)
    u2, u3 = [
        pl.pallas_call(
            functools.partial(project_kernel, d, d == 3),
            out_shape=chunk,
            in_specs=[VM] * 3,
            out_specs=VM,
            compiler_params=LIMIT,
            name=f"project_{d}",
        )(x, m, basis)
        for d, m in ((2, m2), (3, m3))
    ]
    products = shape((nblk, members, LANES), F32)
    weights = shape((nmem, NCODE, LANES), F32)
    uend, wall, e, o = pl.pallas_call(
        edges_kernel,
        out_shape=[products, weights, chunk, chunk],
        in_specs=[VM] * 10,
        out_specs=[VM] * 4,
        compiler_params=LIMIT,
        name="edges",
    )(x, u0, u2, u3, wown, m1, m2, m3, basis, turns)
    nb = lax.axis_size("blk")
    oin = lax.ppermute(o, "blk", partner(nb, 1))
    ein = lax.ppermute(e, "blk", partner(nb, 0))
    z, yi = pl.pallas_call(
        inner_kernel,
        out_shape=[shape((4, members, LANES), F32), shape((2, cols, width), F32)],
        in_specs=[VM] * 8,
        out_specs=[VM] * 2,
        scratch_shapes=[pltpu.VMEM((nblk, members, LANES), F32)],
        compiler_params=LIMIT,
        name="inner",
    )(x, uend, m1, m2, wall, left, basis, turns)
    zo = z[:PAIR] + oin
    outs = pl.pallas_call(
        close_kernel,
        out_shape=[shape((cols, width), F32)] + [shape((cols, width), BF16)] * (nmem - 1),
        in_specs=[VM] * 9,
        out_specs=[VM] * nmem,
        scratch_shapes=[pltpu.VMEM((nmem, cols, width), F32)],
        compiler_params=LIMIT,
        name="close",
    )(x, z, zo, ein, oin, wall, left, turns, yi)
    total = outs[0]
    for d in (3, 2, 1):
        total = total + lax.ppermute(outs[d], "mem", crossed(nmem, d)).astype(F32)
    return total


def solution(mesh):
    in_specs = (
        P("mem", "blk"),
        P(None, ("blk", "mem")),
        P(),
        P(),
        P(("blk", "mem")),
        P(("blk", "mem")),
        P(("blk", "mem")),
    )
    out_specs = P(None, ("blk", "mem"))
    return jax.shard_map(body, mesh=mesh, in_specs=in_specs, out_specs=out_specs, check_vma=False)
```
